32 devices in a mesh: tm: 8 (over z, y), tok: 4 (over x, core).
Axes of the slice: x: 2, y: 2, z: 4, core: 2. Of those that a mesh axis runs over, the one named last changes fastest.
Arguments:
- states: float32 [32, 2, 256, 1152], P('tm', None, 'tok'), may hold values from -6 to 6
- noise: bfloat16 [32, 2, 256, 1152], P('tm', None, 'tok'), may hold values from -6 to 6
- x_start: float32 [2, 256, 1152], P(None, 'tok'), may hold values from -6 to 6
- timesteps: int32 [32], P('tm'), may hold values from 50 to 999
- step_mod: float32 [32, 3, 1152], P('tm'), may hold values from -40 to 40
- view_mod: float32 [8, 3, 1152], replicated, may hold values from -2 to 2
- view_ids: int32 [32, 2], P('tm'), may hold values from 0 to 7
- w_qkv: bfloat16 [1152, 3456], replicated, may hold values from -0.1875 to 0.1875
- w_out: bfloat16 [1152, 1152], replicated, may hold values from -0.1875 to 0.1875
Outputs:
- new_states: float32 [32, 2, 256, 1152], P('tm', None, 'tok')
The draws below stay inside these ranges and needn't reach their ends.
All inputs are finite; a program needn't handle non-finite values.
Results may differ from the reference program's by a relative error of at most 0.0017.
Values may be sent and summed in bfloat16 or wider, within the bound.
A program may use at most 128 MiB of HBM per device.

```python
import jax
import jax.numpy as jnp
from jax import lax

D = 1152
HEADS = 16
HEAD_DIM = 72
TOKENS = 256
VIEWS = 2
NVIEW = 8
SWEEPS = 2
WINDOW = 32


def draw_step_mod(key, part):
    shift_key = jax.random.fold_in(key, 11)
    scale_key = jax.random.fold_in(key, 12)
    gate_key = jax.random.fold_in(key, 13)
    shift = 0.5 * jax.random.normal(shift_key, (WINDOW, D), jnp.float32)
    gate = jax.random.normal(gate_key, (WINDOW, D), jnp.float32)
    scale = 0.5 * jax.random.normal(scale_key, (WINDOW, D), jnp.float32)
    return jnp.clip(jnp.stack([shift, scale, gate], axis=1), -40.0, 40.0).astype(jnp.float32)


def set_ends(drawn, key, low, top_value):
    longest = drawn.shape.index(max(drawn.shape))
    spots = []
    for shift in (0, 1):
        where = [jax.random.randint(jax.random.fold_in(key, axis), (), 0, length) for axis, length in enumerate(drawn.shape)]
        where[longest] = (where[longest] + shift) % drawn.shape[longest]
        spots.append(tuple(where))
    return drawn.at[spots[0]].set(low).at[spots[1]].set(top_value)


def block_scale(key, extent, cuts, low, largest):
    level = 1.0
    for dim, blocks in cuts:
        steps = jax.random.uniform(jax.random.fold_in(jax.random.fold_in(key, 6), dim), (blocks,), jnp.float32, low / len(cuts), largest / len(cuts))
        level = level * jnp.repeat(jnp.exp(steps), extent[dim] // blocks).reshape((-1,) + (1,) * (len(extent) - 1 - dim))
    return level


def scatter_about(own_key, extent, width, limit, cuts=(), dtype=jnp.bfloat16):
    array = width * jax.random.normal(own_key, extent, jnp.float32)
    if cuts:
        array = array * block_scale(own_key, extent, cuts, -0.22, 0.18)
    return jnp.clip(array, -limit, limit).astype(dtype)


def setup_inputs(seed: int = 0) -> dict:
    seeds = jax.random.split(jax.random.key(seed), 10)
    states = scatter_about(seeds[0], (WINDOW, VIEWS, TOKENS, D), 1.0, 6.0, ((0, 8), (2, 4)), jnp.float32)
    noise = scatter_about(seeds[1], (WINDOW, VIEWS, TOKENS, D), 1.0, 6.0, ((0, 8), (2, 4)))
    x_start = scatter_about(seeds[2], (VIEWS, TOKENS, D), 1.0, 6.0, ((1, 4),), jnp.float32)
    timesteps = set_ends(jax.random.randint(seeds[3], (WINDOW,), 50, 1000), jax.random.fold_in(seeds[3], 1), 50, 999).astype(jnp.int32)
    step_mod = draw_step_mod(jax.random.fold_in(seeds[9], 71), 0)
    view_mod = scatter_about(seeds[5], (NVIEW, 3, D), 0.3, 2.0, (), jnp.float32)
    view_ids = set_ends(jax.random.randint(seeds[6], (WINDOW, VIEWS), 0, NVIEW), jax.random.fold_in(seeds[6], 1), 0, NVIEW - 1).astype(jnp.int32)
    w_qkv = scatter_about(seeds[7], (D, 3 * D), D ** -0.5, 0.1875)
    w_out = scatter_about(seeds[8], (D, D), D ** -0.5, 0.1875)
    return dict(states=states, noise=noise, x_start=x_start, timesteps=timesteps, step_mod=step_mod, view_mod=view_mod, view_ids=view_ids, w_qkv=w_qkv, w_out=w_out)


def coefficients(steps_index):
    unit = steps_index.astype(jnp.float32) / 1000.0
    beta = 0.1 + 19.9 * unit
    sigma = jnp.sqrt(1.0 - jnp.exp(-(0.1 * unit + 9.95 * unit * unit)))
    coef_state = 0.5 * beta * 0.004
    coef_eps = beta * 0.004 / sigma
    coef_noise = jnp.sqrt(beta * 0.004)
    return (coef_state, coef_eps, coef_noise)

def increment_of(latent, noise_step, step_index, modulation, w_qkv, w_out):
    center = lax.optimization_barrier(jnp.mean(latent, axis=-1, keepdims=True))
    spread = lax.optimization_barrier(jnp.mean((latent - center) ** 2, axis=-1, keepdims=True))
    normed = (latent - center) / jnp.sqrt(spread + 1e-06)
    modulated = (normed * (1.0 + modulation[:, 1][:, None, :]) + modulation[:, 0][:, None, :]).astype(jnp.bfloat16)
    qkv = jnp.dot(modulated.reshape(-1, D), w_qkv, preferred_element_type=jnp.float32).astype(jnp.bfloat16)
    qkv = qkv.reshape(VIEWS, TOKENS, 3, HEADS, HEAD_DIM).astype(jnp.float32)
    queries = qkv[:, :, 0]
    keys = qkv[:, :, 1]
    values = qkv[:, :, 2]
    scores = jnp.einsum('vqhe,vkhe->vhqk', queries, keys) * (1.0 / HEAD_DIM ** 0.5)
    probs = jax.nn.softmax(scores, axis=-1).astype(jnp.bfloat16)
    attended = jnp.einsum('vhqk,vkhe->vqhe', probs.astype(jnp.float32), values).astype(jnp.bfloat16)
    projected = jnp.dot(attended.reshape(-1, D), w_out, preferred_element_type=jnp.float32).reshape(VIEWS, TOKENS, D)
    denoised = latent + modulation[:, 2][:, None, :] * projected
    coef_state, coef_eps, coef_noise = coefficients(step_index)
    return coef_state * latent + coef_eps * denoised + coef_noise * noise_step.astype(jnp.float32)

def reference(states, noise, x_start, timesteps, step_mod, view_mod, view_ids, w_qkv, w_out):
    modulation = step_mod[:, None] + view_mod[view_ids]
    current = states
    for sweep in range(SWEEPS):
        increments = lax.map(lambda items: increment_of(items[0], items[1], items[2], items[3], w_qkv, w_out), (current, noise, timesteps, modulation))
        running = jnp.cumsum(increments, axis=0)
        before = jnp.concatenate([jnp.zeros_like(running[:1]), running[:-1]], axis=0)
        current = x_start[None] + before
    return current
```

```python
import functools
import math

import jax
import jax.numpy as jnp
from jax import lax
from jax.experimental import pallas as pl
from jax.experimental.pallas import tpu as pltpu
from jax.sharding import PartitionSpec as P

HEADS = 16
SWEEPS = 2
MESH = pl.DeviceIdType.MESH


def coefficients(steps_index):
    unit = steps_index.astype(jnp.float32) / 1000.0
    beta = 0.1 + 19.9 * unit
    sigma = jnp.sqrt(1.0 - jnp.exp(-(0.1 * unit + 9.95 * unit * unit)))
    coef_state = 0.5 * beta * 0.004
    coef_eps = beta * 0.004 / sigma
    coef_noise = jnp.sqrt(beta * 0.004)
    return (coef_state, coef_eps, coef_noise)


def greet(axis, n, me):
    barrier = pltpu.get_barrier_semaphore()
    for k in range(1, n):
        pl.semaphore_signal(
            barrier, inc=1, device_id={axis: lax.rem(me + k, n)}, device_id_type=MESH
        )
    pl.semaphore_wait(barrier, n - 1)


def attend_item(qkv, att, width):
    head = width // HEADS
    tokens = att.shape[0]
    factor = math.log2(math.e) / head**0.5
    for h in range(HEADS):
        lo = (h * head) // 128 * 128
        hi = min(-(-(h + 1) * head // 128) * 128, width)
        span = hi - lo
        lane = lax.broadcasted_iota(jnp.int32, (tokens, span), 1)
        mine = (lane >= h * head - lo) & (lane < (h + 1) * head - lo)
        q = jnp.where(mine, qkv[:, lo:hi], jnp.zeros((), jnp.bfloat16))
        k = qkv[:, width + lo : width + hi]
        v = qkv[:, 2 * width + lo : 2 * width + hi]
        scores = lax.dot_general(
            q, k, (((1,), (1,)), ((), ())), preferred_element_type=jnp.float32
        )
        scores = scores * factor
        top = jnp.max(scores, axis=-1, keepdims=True)
        e = jnp.exp2(scores - top)
        probs = (e * (1.0 / jnp.sum(e, axis=-1, keepdims=True))).astype(jnp.bfloat16)
        o = jnp.dot(probs, v, preferred_element_type=jnp.float32).astype(jnp.bfloat16)
        att[:, lo:hi] = jnp.where(mine, o, att[:, lo:hi])


def attend_kernel(
    n, per, mod_ref, wqkv_hbm, wout_hbm, out_ref,
    wqkv, wout, whole, qkv, att, back, wsem, send1, recv1, send2, recv2,
):
    me = lax.axis_index("tok")
    rows, width = mod_ref.shape[1:]
    load_qkv = pltpu.make_async_copy(wqkv_hbm, wqkv, wsem.at[0])
    load_out = pltpu.make_async_copy(wout_hbm, wout, wsem.at[1])
    load_qkv.start()
    load_out.start()
    greet("tok", n, me)
    sends = []
    for li in range(per):
        for k in range(1, n):
            p = lax.rem(me + k, n)
            c = pltpu.make_async_remote_copy(
                src_ref=mod_ref.at[p * per + li],
                dst_ref=whole.at[li, me],
                send_sem=send1.at[li, k],
                recv_sem=recv1.at[li, me],
                device_id={"tok": p},
                device_id_type=MESH,
            )
            c.start()
            sends.append(c)
    for li in range(per):
        whole[li, me] = mod_ref[me * per + li]
        att[li] = jnp.zeros(att.shape[1:], att.dtype)
    load_qkv.wait()
    for li in range(per):
        for k in range(1, n):
            p = lax.rem(me + k, n)
            pltpu.make_async_remote_copy(
                src_ref=mod_ref.at[p * per + li],
                dst_ref=whole.at[li, p],
                send_sem=send1.at[li, k],
                recv_sem=recv1.at[li, p],
                device_id={"tok": p},
                device_id_type=MESH,
            ).wait_recv()
        x = whole[li].reshape(n * rows, width)
        for c in range(3):
            cols = slice(c * width, (c + 1) * width)
            qkv[:, cols] = jnp.dot(
                x, wqkv[:, cols], preferred_element_type=jnp.float32
            ).astype(jnp.bfloat16)
        attend_item(qkv, att.at[li], width)
        for k in range(1, n):
            p = lax.rem(me + k, n)
            c = pltpu.make_async_remote_copy(
                src_ref=att.at[li, pl.ds(pl.multiple_of(p * rows, rows), rows)],
                dst_ref=back.at[li, me],
                send_sem=send2.at[li, k],
                recv_sem=recv2.at[li, me],
                device_id={"tok": p},
                device_id_type=MESH,
            )
            c.start()
            sends.append(c)
        back[li, me] = att[li, pl.ds(pl.multiple_of(me * rows, rows), rows)]
    load_out.wait()
    for li in range(per):
        for k in range(1, n):
            p = lax.rem(me + k, n)
            pltpu.make_async_remote_copy(
                src_ref=att.at[li, pl.ds(pl.multiple_of(p * rows, rows), rows)],
                dst_ref=back.at[li, p],
                send_sem=send2.at[li, k],
                recv_sem=recv2.at[li, p],
                device_id={"tok": p},
                device_id_type=MESH,
            ).wait_recv()
        y = jnp.dot(
            back[li].reshape(n * rows, width), wout[...], preferred_element_type=jnp.float32
        ).reshape(n, rows, width)
        for p in range(n):
            out_ref[p * per + li] = y[p]
    for c in sends:
        c.wait_send()


def attend(flat_rows, w_qkv, w_out, n):
    items, rows, width = flat_rows.shape
    per = items // n
    vmem = pl.BlockSpec(memory_space=pltpu.VMEM)
    hbm = pl.BlockSpec(memory_space=pl.ANY)
    bf16 = jnp.bfloat16
    return pl.pallas_call(
        functools.partial(attend_kernel, n, per),
        out_shape=jax.ShapeDtypeStruct((items, rows, width), jnp.float32),
        in_specs=[vmem, hbm, hbm],
        out_specs=vmem,
        scratch_shapes=[
            pltpu.VMEM(w_qkv.shape, bf16),
            pltpu.VMEM(w_out.shape, bf16),
            pltpu.VMEM((per, n, rows, width), bf16),
            pltpu.VMEM((n * rows, 3 * width), bf16),
            pltpu.VMEM((per, n * rows, width), bf16),
            pltpu.VMEM((per, n, rows, width), bf16),
            pltpu.SemaphoreType.DMA((2,)),
            pltpu.SemaphoreType.DMA((per, n)),
            pltpu.SemaphoreType.DMA((per, n)),
            pltpu.SemaphoreType.DMA((per, n)),
            pltpu.SemaphoreType.DMA((per, n)),
        ],
        compiler_params=pltpu.CompilerParams(
            collective_id=0, has_side_effects=True, vmem_limit_bytes=48 * 2**20
        ),
        name="attend",
    )(flat_rows, w_qkv, w_out)


def scan_kernel(n, tot_ref, out_ref, got, pre, send1, recv1, send2, recv2):
    me = lax.axis_index("tm")
    greet("tm", n, me)
    sends = []
    for k in range(1, n):
        p = lax.rem(me + k, n)
        c = pltpu.make_async_remote_copy(
            src_ref=tot_ref.at[p],
            dst_ref=got.at[me],
            send_sem=send1.at[k],
            recv_sem=recv1.at[me],
            device_id={"tm": p},
            device_id_type=MESH,
        )
        c.start()
        sends.append(c)
    got[me] = tot_ref[me]
    for k in range(1, n):
        p = lax.rem(me + k, n)
        pltpu.make_async_remote_copy(
            src_ref=tot_ref.at[p],
            dst_ref=got.at[p],
            send_sem=send1.at[k],
            recv_sem=recv1.at[p],
            device_id={"tm": p},
            device_id_type=MESH,
        ).wait_recv()
    run = jnp.zeros(got.shape[1:], got.dtype)
    for r in range(n):
        pre[r] = run
        if r < n - 1:
            run = run + got[r]
    for k in range(1, n):
        p = lax.rem(me + k, n)
        c = pltpu.make_async_remote_copy(
            src_ref=pre.at[p],
            dst_ref=out_ref.at[me],
            send_sem=send2.at[k],
            recv_sem=recv2.at[me],
            device_id={"tm": p},
            device_id_type=MESH,
        )
        c.start()
        sends.append(c)
    out_ref[me] = pre[me]
    for k in range(1, n):
        p = lax.rem(me + k, n)
        pltpu.make_async_remote_copy(
            src_ref=pre.at[p],
            dst_ref=out_ref.at[p],
            send_sem=send2.at[k],
            recv_sem=recv2.at[p],
            device_id={"tm": p},
            device_id_type=MESH,
        ).wait_recv()
    for c in sends:
        c.wait_send()


def lower_sum_of(total, n):
    shape = total.shape
    width = shape[-1]
    chunk = math.prod(shape[:-1]) // n
    vmem = pl.BlockSpec(memory_space=pltpu.VMEM)
    block = (n, chunk, width)
    out = pl.pallas_call(
        functools.partial(scan_kernel, n),
        out_shape=jax.ShapeDtypeStruct(block, total.dtype),
        in_specs=[vmem],
        out_specs=vmem,
        scratch_shapes=[
            pltpu.VMEM(block, total.dtype),
            pltpu.VMEM(block, total.dtype),
            pltpu.SemaphoreType.DMA((n,)),
            pltpu.SemaphoreType.DMA((n,)),
            pltpu.SemaphoreType.DMA((n,)),
            pltpu.SemaphoreType.DMA((n,)),
        ],
        compiler_params=pltpu.CompilerParams(
            collective_id=1, has_side_effects=True, vmem_limit_bytes=32 * 2**20
        ),
        name="lower_sum",
    )(total.reshape(block))
    return out.reshape(shape)


def increments_of(latent, noise, modulation, factors, w_qkv, w_out, n_tok):
    steps_here, views, tok_rows, width = latent.shape
    center = jnp.mean(latent, axis=-1, keepdims=True)
    spread = jnp.mean((latent - center) ** 2, axis=-1, keepdims=True)
    normed = (latent - center) / jnp.sqrt(spread + 1e-06)
    modulated = (
        normed * (1.0 + modulation[:, :, 1][:, :, None, :]) + modulation[:, :, 0][:, :, None, :]
    ).astype(jnp.bfloat16)
    flat_rows = modulated.reshape(steps_here * views, tok_rows, width)
    projected = attend(flat_rows, w_qkv, w_out, n_tok).reshape(latent.shape)
    denoised = latent + modulation[:, :, 2][:, :, None, :] * projected
    coef_state, coef_eps, coef_noise = factors
    return coef_state * latent + coef_eps * denoised + coef_noise * noise.astype(jnp.float32)


def per_device(n_tm, n_tok, states, noise, x_start, timesteps, step_mod, view_mod, view_ids, w_qkv, w_out):
    table_rows = view_mod.shape[0]
    selector = (
        view_ids[:, :, None] == jnp.arange(table_rows, dtype=jnp.int32)[None, None, :]
    ).astype(jnp.float32)
    view_terms = jnp.einsum("svn,ncd->svcd", selector, view_mod, precision=lax.Precision.HIGHEST)
    modulation = step_mod[:, None] + view_terms
    coef_state, coef_eps, coef_noise = coefficients(timesteps)
    factors = (
        coef_state[:, None, None, None],
        coef_eps[:, None, None, None],
        coef_noise[:, None, None, None],
    )
    current = states
    for sweep in range(SWEEPS):
        inc = increments_of(current, noise, modulation, factors, w_qkv, w_out, n_tok)
        lower = lower_sum_of(jnp.sum(inc, axis=0), n_tm)
        running = jnp.cumsum(inc, axis=0)
        before = jnp.concatenate([jnp.zeros_like(running[:1]), running[:-1]], axis=0)
        current = x_start[None] + (lower[None] + before)
    return current


def solution(mesh):
    return jax.shard_map(
        functools.partial(per_device, mesh.shape["tm"], mesh.shape["tok"]),
        mesh=mesh,
        in_specs=(
            P("tm", None, "tok", None),
            P("tm", None, "tok", None),
            P(None, "tok", None),
            P("tm"),
            P("tm", None, None),
            P(),
            P("tm", None),
            P(),
            P(),
        ),
        out_specs=P("tm", None, "tok", None),
        check_vma=False,
    )
```

```python
import functools
import math

import jax
import jax.numpy as jnp
from jax import lax
from jax.experimental import pallas as pl
from jax.experimental.pallas import tpu as pltpu
from jax.sharding import PartitionSpec as P

HEADS = 16
SWEEPS = 2
MESH = pl.DeviceIdType.MESH


def coefficients(steps_index):
    unit = steps_index.astype(jnp.float32) / 1000.0
    beta = 0.1 + 19.9 * unit
    sigma = jnp.sqrt(1.0 - jnp.exp(-(0.1 * unit + 9.95 * unit * unit)))
    coef_state = 0.5 * beta * 0.004
    coef_eps = beta * 0.004 / sigma
    coef_noise = jnp.sqrt(beta * 0.004)
    return (coef_state, coef_eps, coef_noise)


def greet(axes):
    barrier = pltpu.get_barrier_semaphore()
    count = 0
    for axis, n in axes:
        me = lax.axis_index(axis)
        for k in range(1, n):
            pl.semaphore_signal(
                barrier, inc=1, device_id={axis: lax.rem(me + k, n)}, device_id_type=MESH
            )
        count += n - 1
    pl.semaphore_wait(barrier, count)


class Exchange:
    def __init__(self, axis, n, source, dest, send, recv):
        self.axis, self.n, self.source, self.dest = axis, n, source, dest
        self.send, self.recv = send, recv
        self.me = lax.axis_index(axis)

    def copy(self, k, landing):
        p = lax.rem(self.me + k, self.n)
        slot = p if landing else self.me
        return pltpu.make_async_remote_copy(
            src_ref=self.source(p),
            dst_ref=self.dest(slot),
            send_sem=self.send.at[k],
            recv_sem=self.recv.at[slot],
            device_id={self.axis: p},
            device_id_type=MESH,
        )

    def start(self):
        for k in range(1, self.n):
            self.copy(k, False).start()

    def wait_recv(self):
        for k in range(1, self.n):
            self.copy(k, True).wait_recv()

    def wait_send(self):
        for k in range(1, self.n):
            self.copy(k, False).wait_send()


def attend_item(qkv, att, width):
    head = width // HEADS
    tokens = att.shape[0]
    factor = math.log2(math.e) / head**0.5
    for h in range(HEADS):
        lo = (h * head) // 128 * 128
        hi = min(-(-(h + 1) * head // 128) * 128, width)
        span = hi - lo
        lane = lax.broadcasted_iota(jnp.int32, (tokens, span), 1)
        mine = (lane >= h * head - lo) & (lane < (h + 1) * head - lo)
        q = jnp.where(mine, qkv[:, lo:hi], jnp.zeros((), jnp.bfloat16))
        k = qkv[:, width + lo : width + hi]
        v = qkv[:, 2 * width + lo : 2 * width + hi]
        scores = lax.dot_general(
            q, k, (((1,), (1,)), ((), ())), preferred_element_type=jnp.float32
        )
        scores = scores * factor
        top = jnp.max(scores, axis=-1, keepdims=True)
        e = jnp.exp2(scores - top)
        probs = (e * (1.0 / jnp.sum(e, axis=-1, keepdims=True))).astype(jnp.bfloat16)
        o = jnp.dot(probs, v, preferred_element_type=jnp.float32).astype(jnp.bfloat16)
        att[:, lo:hi] = jnp.where(mine, o, att[:, lo:hi])


def modulate(x, scale, shift):
    center = jnp.mean(x, axis=-1, keepdims=True)
    x = x - center
    spread = jnp.mean(x * x, axis=-1, keepdims=True)
    return (x * lax.rsqrt(spread + 1e-06) * (1.0 + scale) + shift).astype(jnp.bfloat16)


def sweeps_kernel(
    n_tm, n_tok, states_hbm, noise_hbm, start_hbm, wqkv_hbm, wout_hbm, mod_ref, lin_ref,
    out_hbm,
    wqkv, wout, lat, noise, start, mod, whole, qkv, att, back, proj, tot, got, pre, low,
    wsem, lsem, osem, s_in, r_in, s_back, r_back, s_up, r_up, s_down, r_down,
):
    me = lax.axis_index("tok")
    my_tm = lax.axis_index("tm")
    steps, views, rows, width = lat.shape
    items = steps * views
    per = items // n_tok
    chunk = tot.shape[-2]
    pieces = [[v] for v in range(views)] if per == views else [list(range(views))]
    groups = [[v] for v in range(views)] if per == views else [list(range(per))]

    loads = []
    for v in range(views):
        c = pltpu.make_async_copy(states_hbm.at[:, v], lat.at[:, v], lsem.at[v])
        c.start()
        loads.append(c)
    load_qkv = pltpu.make_async_copy(wqkv_hbm, wqkv, wsem.at[0])
    load_out = pltpu.make_async_copy(wout_hbm, wout, wsem.at[1])
    load_noise = pltpu.make_async_copy(noise_hbm, noise, wsem.at[2])
    load_start = pltpu.make_async_copy(start_hbm, start, wsem.at[3])
    for c in (load_qkv, load_out, load_noise, load_start):
        c.start()
    greet((("tok", n_tok), ("tm", n_tm)))

    done = []

    def go(exchange):
        exchange.start()
        done.append(exchange)
        return exchange

    def block(buf, sweep, li):
        return lambda p: buf.at[sweep, li, pl.ds(pl.multiple_of(p * rows, rows), rows)]

    def send_in(sweep, piece):
        for v in pieces[piece]:
            for s in range(steps):
                mod[sweep, s * views + v] = modulate(
                    lat[s, v], mod_ref[s, v, 1:2], mod_ref[s, v, 0:1]
                )
        flights = []
        for li in groups[piece]:
            flights.append(go(Exchange(
                "tok", n_tok,
                lambda p, li=li: mod.at[sweep, p * per + li],
                block(whole, sweep, li),
                s_in.at[sweep, li], r_in.at[sweep, li],
            )))
            whole[sweep, li, pl.ds(pl.multiple_of(me * rows, rows), rows)] = mod[
                sweep, me * per + li
            ]
        return flights

    incoming = []
    for piece in range(len(pieces)):
        for v in pieces[piece]:
            loads[v].wait()
        incoming += send_in(0, piece)
    load_qkv.wait()
    for sweep in range(SWEEPS):
        returns = []
        for li in range(per):
            incoming[li].wait_recv()
            for c in range(3):
                cols = slice(c * width, (c + 1) * width)
                qkv[:, cols] = jnp.dot(
                    whole[sweep, li], wqkv[:, cols], preferred_element_type=jnp.float32
                ).astype(jnp.bfloat16)
            att[sweep, li] = jnp.zeros(att.shape[2:], att.dtype)
            attend_item(qkv, att.at[sweep, li], width)
            returns.append(go(Exchange(
                "tok", n_tok, block(att, sweep, li), block(back, sweep, li),
                s_back.at[sweep, li], r_back.at[sweep, li],
            )))
            mine = pl.ds(pl.multiple_of(me * rows, rows), rows)
            back[sweep, li, mine] = att[sweep, li, mine]
        if sweep == 0:
            load_out.wait()
            load_noise.wait()
            load_start.wait()
        ups = []
        for piece in range(len(pieces)):
            for li in groups[piece]:
                returns[li].wait_recv()
                y = jnp.dot(back[sweep, li], wout[...], preferred_element_type=jnp.float32)
                for p in range(n_tok):
                    s, v = divmod(p * per + li, views)
                    proj[s, v] = y[p * rows : (p + 1) * rows]
            for at, v in enumerate(pieces[piece]):
                run = jnp.zeros((rows, width), jnp.float32)
                for s in range(steps):
                    inc = (
                        lin_ref[0, s] * lat[s, v]
                        + mod_ref[s, v, 2:3] * proj[s, v]
                        + lin_ref[1, s] * noise[s, v].astype(jnp.float32)
                    )
                    proj[s, v] = run
                    run = run + inc
                for r in range(rows // chunk):
                    tot[sweep, piece, at * (rows // chunk) + r] = run[
                        r * chunk : (r + 1) * chunk
                    ]
            ups.append(go(Exchange(
                "tm", n_tm,
                lambda p, piece=piece: tot.at[sweep, piece, p],
                lambda p, piece=piece: got.at[sweep, piece, p],
                s_up.at[sweep, piece], r_up.at[sweep, piece],
            )))
            got[sweep, piece, my_tm] = tot[sweep, piece, my_tm]
        downs = []
        for piece in range(len(pieces)):
            ups[piece].wait_recv()
            run = jnp.zeros((chunk, width), jnp.float32)
            for r in range(n_tm):
                pre[sweep, piece, r] = run
                if r < n_tm - 1:
                    run = run + got[sweep, piece, r]
            downs.append(go(Exchange(
                "tm", n_tm,
                lambda p, piece=piece: pre.at[sweep, piece, p],
                lambda p, piece=piece: low.at[sweep, piece, p],
                s_down.at[sweep, piece], r_down.at[sweep, piece],
            )))
            low[sweep, piece, my_tm] = pre[sweep, piece, my_tm]
        incoming = []
        outs = []
        for piece in range(len(pieces)):
            downs[piece].wait_recv()
            for at, v in enumerate(pieces[piece]):
                for r in range(rows // chunk):
                    part = slice(r * chunk, (r + 1) * chunk)
                    lower = low[sweep, piece, at * (rows // chunk) + r]
                    for s in range(steps):
                        lat[s, v, part] = start[v, part] + (lower + proj[s, v, part])
            if sweep < SWEEPS - 1:
                incoming += send_in(sweep + 1, piece)
            else:
                for v in pieces[piece]:
                    c = pltpu.make_async_copy(lat.at[:, v], out_hbm.at[:, v], osem.at[v])
                    c.start()
                    outs.append(c)
    for exchange in done:
        exchange.wait_send()
    for c in outs:
        c.wait()


def run_sweeps(n_tm, n_tok, states, noise, x_start, w_qkv, w_out, modulation, linear):
    steps, views, rows, width = states.shape
    items = steps * views
    per = items // n_tok
    n_pieces = views if per == views else 1
    chunk = views * rows // n_pieces // n_tm
    vmem = pl.BlockSpec(memory_space=pltpu.VMEM)
    smem = pl.BlockSpec(memory_space=pltpu.SMEM)
    hbm = pl.BlockSpec(memory_space=pl.ANY)
    bf16, f32 = jnp.bfloat16, jnp.float32
    dma = pltpu.SemaphoreType.DMA
    tokens = n_tok * rows
    scan = pltpu.VMEM((SWEEPS, n_pieces, n_tm, chunk, width), f32)
    passed = pltpu.VMEM((SWEEPS, per, tokens, width), bf16)
    return pl.pallas_call(
        functools.partial(sweeps_kernel, n_tm, n_tok),
        out_shape=jax.ShapeDtypeStruct(states.shape, f32),
        in_specs=[hbm] * 5 + [vmem, smem],
        out_specs=hbm,
        scratch_shapes=[
            pltpu.VMEM(w_qkv.shape, bf16),
            pltpu.VMEM(w_out.shape, bf16),
            pltpu.VMEM(states.shape, f32),
            pltpu.VMEM(noise.shape, bf16),
            pltpu.VMEM(x_start.shape, f32),
            pltpu.VMEM((SWEEPS, items, rows, width), bf16),
            passed,
            pltpu.VMEM((tokens, 3 * width), bf16),
            passed,
            passed,
            pltpu.VMEM(states.shape, f32),
            scan,
            scan,
            scan,
            scan,
            dma((4,)),
            dma((views,)),
            dma((views,)),
            dma((SWEEPS, per, n_tok)),
            dma((SWEEPS, per, n_tok)),
            dma((SWEEPS, per, n_tok)),
            dma((SWEEPS, per, n_tok)),
            dma((SWEEPS, n_pieces, n_tm)),
            dma((SWEEPS, n_pieces, n_tm)),
            dma((SWEEPS, n_pieces, n_tm)),
            dma((SWEEPS, n_pieces, n_tm)),
        ],
        compiler_params=pltpu.CompilerParams(
            collective_id=0, has_side_effects=True, vmem_limit_bytes=58 * 2**20
        ),
        name="sweeps",
    )(states, noise, x_start, w_qkv, w_out, modulation, linear)


def per_device(n_tm, n_tok, states, noise, x_start, timesteps, step_mod, view_mod, view_ids, w_qkv, w_out):
    table_rows = view_mod.shape[0]
    selector = (
        view_ids[:, :, None] == jnp.arange(table_rows, dtype=jnp.int32)[None, None, :]
    ).astype(jnp.float32)
    view_terms = jnp.einsum("svn,ncd->svcd", selector, view_mod, precision=lax.Precision.HIGHEST)
    modulation = step_mod[:, None] + view_terms
    coef_state, coef_eps, coef_noise = coefficients(timesteps)
    weight = jnp.concatenate(
        [jnp.ones((timesteps.shape[0], 2), jnp.float32), coef_eps[:, None]], axis=1
    )
    modulation = modulation * weight[:, None, :, None]
    linear = jnp.stack([coef_state + coef_eps, coef_noise])
    return run_sweeps(n_tm, n_tok, states, noise, x_start, w_qkv, w_out, modulation, linear)


def solution(mesh):
    return jax.shard_map(
        functools.partial(per_device, mesh.shape["tm"], mesh.shape["tok"]),
        mesh=mesh,
        in_specs=(
            P("tm", None, "tok", None),
            P("tm", None, "tok", None),
            P(None, "tok", None),
            P("tm"),
            P("tm", None, None),
            P(),
            P("tm", None),
            P(),
            P(),
        ),
        out_specs=P("tm", None, "tok", None),
        check_vma=False,
    )
```

```python
import functools
import math

import jax
import jax.numpy as jnp
from jax import lax
from jax.experimental import pallas as pl
from jax.experimental.pallas import tpu as pltpu
from jax.sharding import PartitionSpec as P

HEADS = 16
SWEEPS = 2
MESH = pl.DeviceIdType.MESH


def coefficients(steps_index):
    unit = steps_index.astype(jnp.float32) / 1000.0
    beta = 0.1 + 19.9 * unit
    sigma = jnp.sqrt(1.0 - jnp.exp(-(0.1 * unit + 9.95 * unit * unit)))
    coef_state = 0.5 * beta * 0.004
    coef_eps = beta * 0.004 / sigma
    coef_noise = jnp.sqrt(beta * 0.004)
    return (coef_state, coef_eps, coef_noise)


def greet(n_tok, inner, outer):
    barrier = pltpu.get_barrier_semaphore()
    me, my_tm = lax.axis_index("tok"), lax.axis_index("tm")
    o, i = lax.div(my_tm, inner), lax.rem(my_tm, inner)

    def signal(axis, index):
        pl.semaphore_signal(barrier, inc=1, device_id={axis: index}, device_id_type=MESH)

    for k in range(1, n_tok):
        signal("tok", lax.rem(me + k, n_tok))
    for k in range(1, inner):
        signal("tm", o * inner + lax.rem(i + k, inner))

    @pl.when(o > 0)
    def _():
        signal("tm", my_tm - inner)

    @pl.when(o < outer - 1)
    def _():
        signal("tm", my_tm + inner)

    count = n_tok - 1 + inner - 1
    at_end = (o == 0) | (o == outer - 1)

    @pl.when(at_end)
    def _():
        pl.semaphore_wait(barrier, count + min(outer - 1, 1))

    @pl.when(jnp.logical_not(at_end))
    def _():
        pl.semaphore_wait(barrier, count + 2)


class Exchange:
    def __init__(self, axis, n, source, dest, send, recv):
        self.axis, self.n, self.source, self.dest = axis, n, source, dest
        self.send, self.recv = send, recv
        index = lax.axis_index(axis)
        self.me = lax.rem(index, n)
        self.first = index - self.me

    def copy(self, k, landing):
        p = lax.rem(self.me + k, self.n)
        slot = p if landing else self.me
        return pltpu.make_async_remote_copy(
            src_ref=self.source(p),
            dst_ref=self.dest(slot),
            send_sem=self.send.at[k],
            recv_sem=self.recv.at[slot],
            device_id={self.axis: self.first + p},
            device_id_type=MESH,
        )

    def start(self):
        for k in range(1, self.n):
            self.copy(k, False).start()

    def wait_recv(self):
        for k in range(1, self.n):
            self.copy(k, True).wait_recv()

    def wait_send(self):
        for k in range(1, self.n):
            self.copy(k, False).wait_send()


def attend_item(qkv, att, width):
    head = width // HEADS
    tokens = att.shape[0]
    factor = math.log2(math.e) / head**0.5
    for h in range(HEADS):
        lo = (h * head) // 128 * 128
        hi = min(-(-(h + 1) * head // 128) * 128, width)
        span = hi - lo
        lane = lax.broadcasted_iota(jnp.int32, (tokens, span), 1)
        mine = (lane >= h * head - lo) & (lane < (h + 1) * head - lo)
        q = jnp.where(mine, qkv[:, lo:hi], jnp.zeros((), jnp.bfloat16))
        k = qkv[:, width + lo : width + hi]
        v = qkv[:, 2 * width + lo : 2 * width + hi]
        scores = lax.dot_general(
            q, k, (((1,), (1,)), ((), ())), preferred_element_type=jnp.float32
        )
        scores = scores * factor
        top = jnp.max(scores, axis=-1, keepdims=True)
        e = jnp.exp2(scores - top)
        probs = (e * (1.0 / jnp.sum(e, axis=-1, keepdims=True))).astype(jnp.bfloat16)
        o = jnp.dot(probs, v, preferred_element_type=jnp.float32).astype(jnp.bfloat16)
        att[:, lo:hi] = jnp.where(mine, o, att[:, lo:hi])


def modulate(x, scale, shift):
    center = jnp.mean(x, axis=-1, keepdims=True)
    x = x - center
    spread = jnp.mean(x * x, axis=-1, keepdims=True)
    return (x * lax.rsqrt(spread + 1e-06) * (1.0 + scale) + shift).astype(jnp.bfloat16)


def sweeps_kernel(
    inner, outer, n_tok, states_hbm, noise_hbm, start_hbm, wqkv_hbm, wout_hbm, mod_ref, lin_ref,
    out_hbm,
    wqkv, wout, lat, noise, start, mod, whole, qkv, att, back, proj, tot, got, base, ahead, pre, low,
    wsem, lsem, osem, s_in, r_in, s_back, r_back, s_up, r_up, s_on, r_on, s_down, r_down,
):
    me = lax.axis_index("tok")
    my_tm = lax.axis_index("tm")
    my_outer, my_inner = lax.div(my_tm, inner), lax.rem(my_tm, inner)
    steps, views, rows, width = lat.shape
    items = steps * views
    per = items // n_tok
    cuts, chunk = tot.shape[3:5]
    pieces = [[v] for v in range(views)] if per == views else [list(range(views))]
    groups = [[v] for v in range(views)] if per == views else [list(range(per))]

    loads = []
    for v in range(views):
        c = pltpu.make_async_copy(states_hbm.at[:, v], lat.at[:, v], lsem.at[v])
        c.start()
        loads.append(c)
    load_qkv = pltpu.make_async_copy(wqkv_hbm, wqkv, wsem.at[0])
    load_out = pltpu.make_async_copy(wout_hbm, wout, wsem.at[1])
    load_noise = pltpu.make_async_copy(noise_hbm, noise, wsem.at[2])
    load_start = pltpu.make_async_copy(start_hbm, start, wsem.at[3])
    for c in (load_qkv, load_out, load_noise, load_start):
        c.start()
    greet(n_tok, inner, outer)

    done = []

    def go(exchange):
        exchange.start()
        done.append(exchange)
        return exchange

    def onward(sweep, piece, c):
        return pltpu.make_async_remote_copy(
            src_ref=ahead.at[sweep, piece, c],
            dst_ref=base.at[sweep, piece, c],
            send_sem=s_on.at[sweep, piece, c],
            recv_sem=r_on.at[sweep, piece, c],
            device_id={"tm": my_tm + inner},
            device_id_type=MESH,
        )

    def block(buf, sweep, li):
        return lambda p: buf.at[sweep, li, pl.ds(pl.multiple_of(p * rows, rows), rows)]

    def send_in(sweep, piece):
        for v in pieces[piece]:
            for s in range(steps):
                mod[sweep, s * views + v] = modulate(
                    lat[s, v], mod_ref[s, v, 1:2], mod_ref[s, v, 0:1]
                )
        flights = []
        for li in groups[piece]:
            flights.append(go(Exchange(
                "tok", n_tok,
                lambda p, li=li: mod.at[sweep, p * per + li],
                block(whole, sweep, li),
                s_in.at[sweep, li], r_in.at[sweep, li],
            )))
            whole[sweep, li, pl.ds(pl.multiple_of(me * rows, rows), rows)] = mod[
                sweep, me * per + li
            ]
        return flights

    incoming = []
    for piece in range(len(pieces)):
        for v in pieces[piece]:
            loads[v].wait()
        incoming += send_in(0, piece)
    load_qkv.wait()
    for sweep in range(SWEEPS):
        returns = []
        for li in range(per):
            incoming[li].wait_recv()
            for c in range(3):
                cols = slice(c * width, (c + 1) * width)
                qkv[:, cols] = jnp.dot(
                    whole[sweep, li], wqkv[:, cols], preferred_element_type=jnp.float32
                ).astype(jnp.bfloat16)
            att[sweep, li] = jnp.zeros(att.shape[2:], att.dtype)
            attend_item(qkv, att.at[sweep, li], width)
            returns.append(go(Exchange(
                "tok", n_tok, block(att, sweep, li), block(back, sweep, li),
                s_back.at[sweep, li], r_back.at[sweep, li],
            )))
            mine = pl.ds(pl.multiple_of(me * rows, rows), rows)
            back[sweep, li, mine] = att[sweep, li, mine]
        if sweep == 0:
            load_out.wait()
            load_noise.wait()
            load_start.wait()
        ups = []
        for piece in range(len(pieces)):
            for li in groups[piece]:
                returns[li].wait_recv()
                y = jnp.dot(back[sweep, li], wout[...], preferred_element_type=jnp.float32)
                for p in range(n_tok):
                    s, v = divmod(p * per + li, views)
                    proj[s, v] = y[p * rows : (p + 1) * rows]
            for at, v in enumerate(pieces[piece]):
                run = jnp.zeros((rows, width), jnp.float32)
                for s in range(steps):
                    inc = (
                        lin_ref[0, s] * lat[s, v]
                        + mod_ref[s, v, 2:3] * proj[s, v]
                        + lin_ref[1, s] * noise[s, v].astype(jnp.float32)
                    )
                    proj[s, v] = run
                    run = run + inc
                for r in range(rows // chunk):
                    i, c = divmod(at * (rows // chunk) + r, cuts)
                    tot[sweep, piece, i, c] = run[r * chunk : (r + 1) * chunk]
            for c in range(cuts):
                ups.append(go(Exchange(
                    "tm", inner,
                    lambda p, piece=piece, c=c: tot.at[sweep, piece, p, c],
                    lambda p, piece=piece, c=c: got.at[sweep, piece, p, c],
                    s_up.at[sweep, piece, c], r_up.at[sweep, piece, c],
                )))
            got[sweep, piece, my_inner] = tot[sweep, piece, my_inner]
        downs = []
        for piece in range(len(pieces)):
            for c in range(cuts):
                ups[piece * cuts + c].wait_recv()
                parts = [got[sweep, piece, i, c] for i in range(inner)]

                @pl.when(my_outer == 0)
                def _():
                    base[sweep, piece, c] = jnp.zeros((chunk, width), jnp.float32)

                @pl.when(my_outer > 0)
                def _():
                    onward(sweep, piece, c).wait_recv()

                run = base[sweep, piece, c]
                for i in range(inner):
                    pre[sweep, piece, i, c] = run
                    run = run + parts[i]
                ahead[sweep, piece, c] = run

                @pl.when(my_outer < outer - 1)
                def _():
                    onward(sweep, piece, c).start()

                downs.append(go(Exchange(
                    "tm", inner,
                    lambda p, piece=piece, c=c: pre.at[sweep, piece, p, c],
                    lambda p, piece=piece, c=c: low.at[sweep, piece, p, c],
                    s_down.at[sweep, piece, c], r_down.at[sweep, piece, c],
                )))
                low[sweep, piece, my_inner, c] = pre[sweep, piece, my_inner, c]
        incoming = []
        outs = []
        for piece in range(len(pieces)):
            for c in range(cuts):
                downs[piece * cuts + c].wait_recv()
            for at, v in enumerate(pieces[piece]):
                for r in range(rows // chunk):
                    part = slice(r * chunk, (r + 1) * chunk)
                    i, c = divmod(at * (rows // chunk) + r, cuts)
                    lower = low[sweep, piece, i, c]
                    for s in range(steps):
                        lat[s, v, part] = start[v, part] + (lower + proj[s, v, part])
            if sweep < SWEEPS - 1:
                incoming += send_in(sweep + 1, piece)
            else:
                for v in pieces[piece]:
                    c = pltpu.make_async_copy(lat.at[:, v], out_hbm.at[:, v], osem.at[v])
                    c.start()
                    outs.append(c)
    for exchange in done:
        exchange.wait_send()

    @pl.when(my_outer < outer - 1)
    def _():
        for sweep in range(SWEEPS):
            for piece in range(len(pieces)):
                for c in range(cuts):
                    onward(sweep, piece, c).wait_send()

    for c in outs:
        c.wait()


def run_sweeps(n_tm, n_tok, states, noise, x_start, w_qkv, w_out, modulation, linear):
    steps, views, rows, width = states.shape
    items = steps * views
    per = items // n_tok
    n_pieces = views if per == views else 1
    inner = 1
    while 4 * inner * inner <= n_tm:
        inner *= 2
    outer = n_tm // inner
    share = views * rows // n_pieces // inner
    cuts = share // 8 if share % 8 == 0 else 1
    chunk = share // cuts
    vmem = pl.BlockSpec(memory_space=pltpu.VMEM)
    smem = pl.BlockSpec(memory_space=pltpu.SMEM)
    hbm = pl.BlockSpec(memory_space=pl.ANY)
    bf16, f32 = jnp.bfloat16, jnp.float32
    dma = pltpu.SemaphoreType.DMA
    tokens = n_tok * rows
    scan = pltpu.VMEM((SWEEPS, n_pieces, inner, cuts, chunk, width), f32)
    link = pltpu.VMEM((SWEEPS, n_pieces, cuts, chunk, width), f32)
    passed = pltpu.VMEM((SWEEPS, per, tokens, width), bf16)
    return pl.pallas_call(
        functools.partial(sweeps_kernel, inner, outer, n_tok),
        out_shape=jax.ShapeDtypeStruct(states.shape, f32),
        in_specs=[hbm] * 5 + [vmem, smem],
        out_specs=hbm,
        scratch_shapes=[
            pltpu.VMEM(w_qkv.shape, bf16),
            pltpu.VMEM(w_out.shape, bf16),
            pltpu.VMEM(states.shape, f32),
            pltpu.VMEM(noise.shape, bf16),
            pltpu.VMEM(x_start.shape, f32),
            pltpu.VMEM((SWEEPS, items, rows, width), bf16),
            passed,
            pltpu.VMEM((tokens, 3 * width), bf16),
            passed,
            passed,
            pltpu.VMEM(states.shape, f32),
            scan,
            scan,
            link,
            link,
            scan,
            scan,
            dma((4,)),
            dma((views,)),
            dma((views,)),
            dma((SWEEPS, per, n_tok)),
            dma((SWEEPS, per, n_tok)),
            dma((SWEEPS, per, n_tok)),
            dma((SWEEPS, per, n_tok)),
            dma((SWEEPS, n_pieces, cuts, inner)),
            dma((SWEEPS, n_pieces, cuts, inner)),
            dma((SWEEPS, n_pieces, cuts)),
            dma((SWEEPS, n_pieces, cuts)),
            dma((SWEEPS, n_pieces, cuts, inner)),
            dma((SWEEPS, n_pieces, cuts, inner)),
        ],
        compiler_params=pltpu.CompilerParams(
            collective_id=0, has_side_effects=True, vmem_limit_bytes=58 * 2**20
        ),
        name="sweeps",
    )(states, noise, x_start, w_qkv, w_out, modulation, linear)


def per_device(n_tm, n_tok, states, noise, x_start, timesteps, step_mod, view_mod, view_ids, w_qkv, w_out):
    table_rows = view_mod.shape[0]
    selector = (
        view_ids[:, :, None] == jnp.arange(table_rows, dtype=jnp.int32)[None, None, :]
    ).astype(jnp.float32)
    view_terms = jnp.einsum("svn,ncd->svcd", selector, view_mod, precision=lax.Precision.HIGHEST)
    modulation = step_mod[:, None] + view_terms
    coef_state, coef_eps, coef_noise = coefficients(timesteps)
    weight = jnp.concatenate(
        [jnp.ones((timesteps.shape[0], 2), jnp.float32), coef_eps[:, None]], axis=1
    )
    modulation = modulation * weight[:, None, :, None]
    linear = jnp.stack([coef_state + coef_eps, coef_noise])
    return run_sweeps(n_tm, n_tok, states, noise, x_start, w_qkv, w_out, modulation, linear)


def solution(mesh):
    return jax.shard_map(
        functools.partial(per_device, mesh.shape["tm"], mesh.shape["tok"]),
        mesh=mesh,
        in_specs=(
            P("tm", None, "tok", None),
            P("tm", None, "tok", None),
            P(None, "tok", None),
            P("tm"),
            P("tm", None, None),
            P(),
            P("tm", None),
            P(),
            P(),
        ),
        out_specs=P("tm", None, "tok", None),
        check_vma=False,
    )
```

```python
import functools
import math

import jax
import jax.numpy as jnp
from jax import lax
from jax.experimental import pallas as pl
from jax.experimental.pallas import tpu as pltpu
from jax.sharding import PartitionSpec as P

HEADS = 16
SWEEPS = 2
MESH = pl.DeviceIdType.MESH


def coefficients(steps_index):
    unit = steps_index.astype(jnp.float32) / 1000.0
    beta = 0.1 + 19.9 * unit
    sigma = jnp.sqrt(1.0 - jnp.exp(-(0.1 * unit + 9.95 * unit * unit)))
    coef_state = 0.5 * beta * 0.004
    coef_eps = beta * 0.004 / sigma
    coef_noise = jnp.sqrt(beta * 0.004)
    return (coef_state, coef_eps, coef_noise)


def greet(n_tok, inner, outer):
    barrier = pltpu.get_barrier_semaphore()
    me, my_tm = lax.axis_index("tok"), lax.axis_index("tm")
    o, i = lax.div(my_tm, inner), lax.rem(my_tm, inner)

    def signal(axis, index):
        pl.semaphore_signal(barrier, inc=1, device_id={axis: index}, device_id_type=MESH)

    for k in range(1, n_tok):
        signal("tok", lax.rem(me + k, n_tok))
    for k in range(1, inner):
        signal("tm", o * inner + lax.rem(i + k, inner))

    @pl.when(o > 0)
    def _():
        signal("tm", my_tm - inner)

    @pl.when(o < outer - 1)
    def _():
        signal("tm", my_tm + inner)

    count = n_tok - 1 + inner - 1
    at_end = (o == 0) | (o == outer - 1)

    @pl.when(at_end)
    def _():
        pl.semaphore_wait(barrier, count + min(outer - 1, 1))

    @pl.when(jnp.logical_not(at_end))
    def _():
        pl.semaphore_wait(barrier, count + 2)


class Exchange:
    def __init__(self, axis, n, source, dest, send, recv):
        self.axis, self.n, self.source, self.dest = axis, n, source, dest
        self.send, self.recv = send, recv
        index = lax.axis_index(axis)
        self.me = lax.rem(index, n)
        self.first = index - self.me

    def copy(self, k, landing):
        p = lax.rem(self.me + k, self.n)
        slot = p if landing else self.me
        return pltpu.make_async_remote_copy(
            src_ref=self.source(p),
            dst_ref=self.dest(slot),
            send_sem=self.send.at[k],
            recv_sem=self.recv.at[slot],
            device_id={self.axis: self.first + p},
            device_id_type=MESH,
        )

    def start(self):
        for k in range(1, self.n):
            self.copy(k, False).start()

    def wait_recv(self):
        for k in range(1, self.n):
            self.copy(k, True).wait_recv()

    def wait_send(self):
        for k in range(1, self.n):
            self.copy(k, False).wait_send()


def attend_item(qkv, att, width):
    head = width // HEADS
    tokens = att.shape[0]
    factor = math.log2(math.e) / head**0.5
    for h in range(HEADS):
        lo = (h * head) // 128 * 128
        hi = min(-(-(h + 1) * head // 128) * 128, width)
        span = hi - lo
        lane = lax.broadcasted_iota(jnp.int32, (tokens, span), 1)
        mine = (lane >= h * head - lo) & (lane < (h + 1) * head - lo)
        q = jnp.where(mine, qkv[:, lo:hi], jnp.zeros((), jnp.bfloat16))
        k = qkv[:, width + lo : width + hi]
        v = qkv[:, 2 * width + lo : 2 * width + hi]
        scores = lax.dot_general(
            q, k, (((1,), (1,)), ((), ())), preferred_element_type=jnp.float32
        )
        scores = scores * factor
        top = jnp.max(scores, axis=-1, keepdims=True)
        e = jnp.exp2(scores - top)
        probs = (e * (1.0 / jnp.sum(e, axis=-1, keepdims=True))).astype(jnp.bfloat16)
        o = jnp.dot(probs, v, preferred_element_type=jnp.float32).astype(jnp.bfloat16)
        att[:, lo:hi] = jnp.where(mine, o, att[:, lo:hi])


def modulate(x, scale, shift):
    center = jnp.mean(x, axis=-1, keepdims=True)
    x = x - center
    spread = jnp.mean(x * x, axis=-1, keepdims=True)
    return (x * lax.rsqrt(spread + 1e-06) * (1.0 + scale) + shift).astype(jnp.bfloat16)


def sweeps_kernel(
    inner, outer, n_tok, states_hbm, noise_hbm, start_hbm, wqkv_hbm, wout_hbm, mod_ref, lin_ref,
    out_hbm,
    wqkv, wout, lat, noise, start, mod, whole, qkv, att, back, proj, tot, got, base, ahead, pre, low,
    wsem, lsem, osem, s_in, r_in, s_back, r_back, s_up, r_up, s_on, r_on, s_down, r_down,
):
    me = lax.axis_index("tok")
    my_tm = lax.axis_index("tm")
    my_outer, my_inner = lax.div(my_tm, inner), lax.rem(my_tm, inner)
    steps, views, rows, width = lat.shape
    items = steps * views
    per = items // n_tok
    cuts, chunk = tot.shape[3:5]
    pieces = [[v] for v in range(views)] if per == views else [list(range(views))]
    groups = [[v] for v in range(views)] if per == views else [list(range(per))]

    loads = []
    for v in range(views):
        c = pltpu.make_async_copy(states_hbm.at[:, v], lat.at[:, v], lsem.at[v])
        c.start()
        loads.append(c)
    load_qkv = pltpu.make_async_copy(wqkv_hbm, wqkv, wsem.at[0])
    load_out = pltpu.make_async_copy(wout_hbm, wout, wsem.at[1])
    load_noise = pltpu.make_async_copy(noise_hbm, noise, wsem.at[2])
    load_start = pltpu.make_async_copy(start_hbm, start, wsem.at[3])
    for c in (load_qkv, load_out, load_noise, load_start):
        c.start()
    greet(n_tok, inner, outer)

    done = []

    def go(exchange):
        exchange.start()
        done.append(exchange)
        return exchange

    def onward(sweep, piece, c):
        return pltpu.make_async_remote_copy(
            src_ref=ahead.at[sweep, piece, c],
            dst_ref=base.at[sweep, piece, c],
            send_sem=s_on.at[sweep, piece, c],
            recv_sem=r_on.at[sweep, piece, c],
            device_id={"tm": my_tm + inner},
            device_id_type=MESH,
        )

    def block(buf, sweep, li):
        return lambda p: buf.at[sweep, li, pl.ds(pl.multiple_of(p * rows, rows), rows)]

    def send_in(sweep, piece):
        for v in pieces[piece]:
            for s in range(steps):
                mod[sweep, s * views + v] = modulate(
                    lat[s, v], mod_ref[s, v, 1:2], mod_ref[s, v, 0:1]
                )
        flights = []
        for li in groups[piece]:
            flights.append(go(Exchange(
                "tok", n_tok,
                lambda p, li=li: mod.at[sweep, p * per + li],
                block(whole, sweep, li),
                s_in.at[sweep, li], r_in.at[sweep, li],
            )))
            whole[sweep, li, pl.ds(pl.multiple_of(me * rows, rows), rows)] = mod[
                sweep, me * per + li
            ]
        return flights

    incoming = []
    for piece in range(len(pieces)):
        for v in pieces[piece]:
            loads[v].wait()
        incoming += send_in(0, piece)
    load_qkv.wait()
    for sweep in range(SWEEPS):
        returns = []
        for li in range(per):
            incoming[li].wait_recv()
            for c in range(3):
                cols = slice(c * width, (c + 1) * width)
                qkv[:, cols] = jnp.dot(
                    whole[sweep, li], wqkv[:, cols], preferred_element_type=jnp.float32
                ).astype(jnp.bfloat16)
            att[sweep, li] = jnp.zeros(att.shape[2:], att.dtype)
            attend_item(qkv, att.at[sweep, li], width)
            returns.append(go(Exchange(
                "tok", n_tok, block(att, sweep, li), block(back, sweep, li),
                s_back.at[sweep, li], r_back.at[sweep, li],
            )))
            mine = pl.ds(pl.multiple_of(me * rows, rows), rows)
            back[sweep, li, mine] = att[sweep, li, mine]
        if sweep == 0:
            load_out.wait()
            load_noise.wait()
            load_start.wait()
        ups = []
        for piece in range(len(pieces)):
            for li in groups[piece]:
                returns[li].wait_recv()
                y = jnp.dot(back[sweep, li], wout[...], preferred_element_type=jnp.float32)
                for p in range(n_tok):
                    s, v = divmod(p * per + li, views)
                    proj[s, v] = y[p * rows : (p + 1) * rows]
            for at, v in enumerate(pieces[piece]):
                run = jnp.zeros((rows, width), jnp.float32)
                for s in range(steps):
                    inc = (
                        lin_ref[0, s] * lat[s, v]
                        + mod_ref[s, v, 2:3] * proj[s, v]
                        + lin_ref[1, s] * noise[s, v].astype(jnp.float32)
                    )
                    proj[s, v] = run
                    run = run + inc
                for r in range(rows // chunk):
                    i, c = divmod(at * (rows // chunk) + r, cuts)
                    tot[sweep, piece, i, c] = run[r * chunk : (r + 1) * chunk]
            for c in range(cuts):
                ups.append(go(Exchange(
                    "tm", inner,
                    lambda p, piece=piece, c=c: tot.at[sweep, piece, p, c],
                    lambda p, piece=piece, c=c: got.at[sweep, piece, p, c],
                    s_up.at[sweep, piece, c], r_up.at[sweep, piece, c],
                )))
            got[sweep, piece, my_inner] = tot[sweep, piece, my_inner]
        downs = []
        for piece in range(len(pieces)):
            for c in range(cuts):
                ups[piece * cuts + c].wait_recv()
                parts = [got[sweep, piece, i, c] for i in range(inner)]

                @pl.when(my_outer == 0)
                def _():
                    base[sweep, piece, c] = jnp.zeros((chunk, width), jnp.float32)

                @pl.when(my_outer > 0)
                def _():
                    onward(sweep, piece, c).wait_recv()

                run = base[sweep, piece, c]
                for i in range(inner):
                    pre[sweep, piece, i, c] = run
                    run = run + parts[i]
                ahead[sweep, piece, c] = run

                @pl.when(my_outer < outer - 1)
                def _():
                    onward(sweep, piece, c).start()

                downs.append(go(Exchange(
                    "tm", inner,
                    lambda p, piece=piece, c=c: pre.at[sweep, piece, p, c],
                    lambda p, piece=piece, c=c: low.at[sweep, piece, p, c],
                    s_down.at[sweep, piece, c], r_down.at[sweep, piece, c],
                )))
                low[sweep, piece, my_inner, c] = pre[sweep, piece, my_inner, c]
        incoming = []
        outs = []
        for piece in range(len(pieces)):
            for c in range(cuts):
                downs[piece * cuts + c].wait_recv()
            for at, v in enumerate(pieces[piece]):
                for r in range(rows // chunk):
                    part = slice(r * chunk, (r + 1) * chunk)
                    i, c = divmod(at * (rows // chunk) + r, cuts)
                    lower = low[sweep, piece, i, c]
                    for s in range(steps):
                        ahead_of = lower + proj[s, v, part]
                        if sweep < SWEEPS - 1:
                            ahead_of = start[v, part] + ahead_of
                        lat[s, v, part] = ahead_of
            if sweep < SWEEPS - 1:
                incoming += send_in(sweep + 1, piece)
            else:
                for v in pieces[piece]:
                    c = pltpu.make_async_copy(lat.at[:, v], out_hbm.at[:, v], osem.at[v])
                    c.start()
                    outs.append(c)
    for exchange in done:
        exchange.wait_send()

    @pl.when(my_outer < outer - 1)
    def _():
        for sweep in range(SWEEPS):
            for piece in range(len(pieces)):
                for c in range(cuts):
                    onward(sweep, piece, c).wait_send()

    for c in outs:
        c.wait()


def run_sweeps(n_tm, n_tok, states, noise, x_start, w_qkv, w_out, modulation, linear):
    steps, views, rows, width = states.shape
    items = steps * views
    per = items // n_tok
    n_pieces = views if per == views else 1
    inner = 1
    while 4 * inner * inner <= n_tm:
        inner *= 2
    outer = n_tm // inner
    share = views * rows // n_pieces // inner
    cuts = share // 8 if share % 8 == 0 else 1
    chunk = share // cuts
    vmem = pl.BlockSpec(memory_space=pltpu.VMEM)
    smem = pl.BlockSpec(memory_space=pltpu.SMEM)
    hbm = pl.BlockSpec(memory_space=pl.ANY)
    bf16, f32 = jnp.bfloat16, jnp.float32
    dma = pltpu.SemaphoreType.DMA
    tokens = n_tok * rows
    scan = pltpu.VMEM((SWEEPS, n_pieces, inner, cuts, chunk, width), f32)
    link = pltpu.VMEM((SWEEPS, n_pieces, cuts, chunk, width), f32)
    passed = pltpu.VMEM((SWEEPS, per, tokens, width), bf16)
    return pl.pallas_call(
        functools.partial(sweeps_kernel, inner, outer, n_tok),
        out_shape=jax.ShapeDtypeStruct(states.shape, f32),
        in_specs=[hbm] * 5 + [vmem, smem],
        out_specs=hbm,
        scratch_shapes=[
            pltpu.VMEM(w_qkv.shape, bf16),
            pltpu.VMEM(w_out.shape, bf16),
            pltpu.VMEM(states.shape, f32),
            pltpu.VMEM(noise.shape, bf16),
            pltpu.VMEM(x_start.shape, f32),
            pltpu.VMEM((SWEEPS, items, rows, width), bf16),
            passed,
            pltpu.VMEM((tokens, 3 * width), bf16),
            passed,
            passed,
            pltpu.VMEM(states.shape, f32),
            scan,
            scan,
            link,
            link,
            scan,
            scan,
            dma((4,)),
            dma((views,)),
            dma((views,)),
            dma((SWEEPS, per, n_tok)),
            dma((SWEEPS, per, n_tok)),
            dma((SWEEPS, per, n_tok)),
            dma((SWEEPS, per, n_tok)),
            dma((SWEEPS, n_pieces, cuts, inner)),
            dma((SWEEPS, n_pieces, cuts, inner)),
            dma((SWEEPS, n_pieces, cuts)),
            dma((SWEEPS, n_pieces, cuts)),
            dma((SWEEPS, n_pieces, cuts, inner)),
            dma((SWEEPS, n_pieces, cuts, inner)),
        ],
        compiler_params=pltpu.CompilerParams(
            collective_id=0, has_side_effects=True, vmem_limit_bytes=58 * 2**20
        ),
        name="sweeps",
    )(states, noise, x_start, w_qkv, w_out, modulation, linear)


def per_device(n_tm, n_tok, states, noise, x_start, timesteps, step_mod, view_mod, view_ids, w_qkv, w_out):
    table_rows = view_mod.shape[0]
    selector = (
        view_ids[:, :, None] == jnp.arange(table_rows, dtype=jnp.int32)[None, None, :]
    ).astype(jnp.float32)
    view_terms = jnp.einsum("svn,ncd->svcd", selector, view_mod, precision=lax.Precision.HIGHEST)
    modulation = step_mod[:, None] + view_terms
    coef_state, coef_eps, coef_noise = coefficients(timesteps)
    weight = jnp.concatenate(
        [jnp.ones((timesteps.shape[0], 2), jnp.float32), coef_eps[:, None]], axis=1
    )
    modulation = modulation * weight[:, None, :, None]
    linear = jnp.stack([coef_state + coef_eps, coef_noise])
    moved = run_sweeps(n_tm, n_tok, states, noise, x_start, w_qkv, w_out, modulation, linear)
    return x_start[None] + moved


def solution(mesh):
    return jax.shard_map(
        functools.partial(per_device, mesh.shape["tm"], mesh.shape["tok"]),
        mesh=mesh,
        in_specs=(
            P("tm", None, "tok", None),
            P("tm", None, "tok", None),
            P(None, "tok", None),
            P("tm"),
            P("tm", None, None),
            P(),
            P("tm", None),
            P(),
            P(),
        ),
        out_specs=P("tm", None, "tok", None),
        check_vma=False,
    )
```
